32 devices in a mesh: groups: 2 (over x), row: 16 (over z, y, core).
Axes of the slice: x: 2, y: 2, z: 4, core: 2. Of those that a mesh axis runs over, the one named last changes fastest.
Arguments:
- object_field: float32 [2, 16384, 384], P(None, ('groups', 'row')), parts along dimension 1, may hold values from -26 to 26
- probe: float32 [2, 2, 256, 256], replicated, may hold values from -4.2 to 4.2
- amplitude: float32 [256, 256, 256], P(('groups', 'row')), parts along dimension 0, may hold values from 0.2 to 27, as said below
- offsets: int32 [256, 2], P(('groups', 'row')), parts along dimension 0, may hold values from 0 to 8191, as said below
Outputs:
- object_grad: float32 [2, 16384, 384], P(None, ('groups', 'row')), parts along dimension 1
- probe_dir: float32 [4, 2, 256, 256], P('groups'), parts along dimension 0
- loss: float32 [2], P('groups'), parts along dimension 0
The draws below stay inside these ranges and needn't reach their ends.
There are 2 independent parts, one for each index of `groups`. The reference program is written for one: setup_inputs(seed, part) draws one part's arguments, and reference() takes and returns one part's arrays. A program takes and returns all parts, laid end to end along the dimension named above; an argument that names none is the same for every part. Nothing has to cross between parts.
Inputs may be any that keep to these rules, and one draw needn't show every extreme that they name: offsets[p, 0] is k * 64 plus a shift below 64 in the rows of device p // 8, with k = p % 8; offsets[p, 1] lies from 0 to 127. `amplitude`: measured amplitudes are positive.
All inputs are finite; a program needn't handle non-finite values.
Results may differ from the reference program's by a relative error of at most 0.0062.
Values sent between devices are 32-bit elements; how exact they have to be, the bound alone decides.
A program may use at most 128 MiB of HBM per device.

```python
import math
import jax
import jax.numpy as jnp
from jax import lax

PATCH = 256
MODES = 2
STEP = 64
TILE = 512
SPAN = 128
OWIDTH = 384
POS_DEV = 8
POSITIONS = 128
NROWS = 8192
N_ROW = 16


def draw_offsets(key, part):
    first_key, second_key = jax.random.split(jax.random.fold_in(key, 11))
    index = jnp.arange(POSITIONS, dtype=jnp.int32)
    device = index // POS_DEV
    within = index % POS_DEV
    row_shift = jax.random.randint(first_key, (POSITIONS,), 0, STEP, dtype=jnp.int32)
    col_start = jax.random.randint(second_key, (POSITIONS,), 0, SPAN, dtype=jnp.int32)
    first = index == 0
    last = index == POSITIONS - 1
    row_shift = jnp.where(first, 0, jnp.where(last, STEP - 1, row_shift))
    col_start = jnp.where(first, 0, jnp.where(last, SPAN - 1, col_start))
    rows = device * TILE + within * STEP + row_shift
    return jnp.stack([rows, col_start], 1).astype(jnp.int32)


def draw_object_field(key, part):
    base_key, row_key, col_key = jax.random.split(jax.random.fold_in(key, 23), 3)
    row_scale = jnp.exp(jax.random.uniform(row_key, (NROWS,), jnp.float32, math.log(0.3), math.log(3.0)))
    col_scale = jnp.exp(jax.random.uniform(col_key, (OWIDTH,), jnp.float32, math.log(0.3), math.log(3.0)))
    scales = row_scale[:, None] * col_scale[None, :]
    base = jnp.clip(jax.random.normal(base_key, (2, NROWS, OWIDTH), jnp.float32), -4.0, 4.0) * 0.7
    return (base * scales[None]).astype(jnp.float32)


def draw_amplitude(key, part):
    base_key = jax.random.fold_in(key, 37)
    where = jnp.arange(POSITIONS, dtype=jnp.int32).astype(jnp.float32) / max(POSITIONS - 1, 1)
    base = jnp.exp(jax.random.uniform(base_key, (POSITIONS, PATCH, PATCH), jnp.float32, math.log(0.3), math.log(3.0)))
    rise = 1.0 + 2.0 * where
    return (base * rise[:, None, None]).astype(jnp.float32)


def normal_values(own_key, dims, width, bound, kind=jnp.bfloat16):
    drawn = width * jax.random.normal(own_key, dims, jnp.float32)
    return jnp.clip(drawn, min=-bound, max=bound).astype(kind)


def setup_inputs(seed: int = 0, part: int = 0) -> dict:
    key_list = jax.random.split(jax.random.key(seed), 5)
    part_splits = jax.random.split(jax.random.fold_in(key_list[4], part), 5)
    return {
        "object_field": draw_object_field(jax.random.fold_in(jax.random.fold_in(key_list[4], part), 71), part),
        "probe": normal_values(key_list[1], (MODES, 2, PATCH, PATCH), 0.7, 4.2, jnp.float32),
        "amplitude": draw_amplitude(jax.random.fold_in(jax.random.fold_in(key_list[4], part), 71), part),
        "offsets": draw_offsets(jax.random.fold_in(jax.random.fold_in(key_list[4], part), 71), part),
    }


def dft_tables(size):
    idx = jnp.arange(size, dtype=jnp.int32)
    prod = idx[:, None] * idx[None, :] % size
    angle = prod.astype(jnp.float32) * (2.0 * math.pi / size)
    scale = 1.0 / math.sqrt(size)
    cosine = jnp.cos(angle) * scale
    sine = jnp.sin(angle) * scale
    column = jnp.stack([jnp.stack([cosine, -sine], 1), jnp.stack([sine, cosine], 1)], 0).astype(jnp.bfloat16)
    rowwise = jnp.stack([jnp.stack([cosine, sine], 1), jnp.stack([-sine, cosine], 1)], 0).astype(jnp.bfloat16)
    return (column, rowwise)

def mix(form, left, right):
    return jnp.einsum(form, left.astype(jnp.float32), right.astype(jnp.float32), precision=lax.Precision.HIGHEST)

def window_terms(windows, probe, amplitude, column, rowwise):
    o_re = windows[:, 0][:, None]
    o_im = windows[:, 1][:, None]
    p_re = probe[:, 0][None]
    p_im = probe[:, 1][None]
    wave = jnp.stack([p_re * o_re - p_im * o_im, p_re * o_im + p_im * o_re], 2).astype(jnp.bfloat16)
    half = mix('pmcij,cjdk->pmdik', wave, column).astype(jnp.bfloat16)
    far = mix('erdi,pmdil->pmerl', rowwise, half)
    magnitude = jnp.sqrt(lax.optimization_barrier(jnp.sum(far * far, axis=(1, 2))))
    loss_part = jnp.sum((magnitude - amplitude) ** 2)
    weight = 0.25 * (1.0 - amplitude / jnp.maximum(magnitude, 0.5))
    grad_far = (weight[:, None, None] * far).astype(jnp.bfloat16)
    grad_half = mix('erdi,pmerl->pmdil', rowwise, grad_far).astype(jnp.bfloat16)
    grad_wave = mix('pmdik,cjdk->pmcij', grad_half, column)
    g_re = grad_wave[:, :, 0]
    g_im = grad_wave[:, :, 1]
    win_grad = jnp.stack([lax.optimization_barrier(jnp.sum(p_re * g_re + p_im * g_im, 1)), lax.optimization_barrier(jnp.sum(p_re * g_im - p_im * g_re, 1))], 1)
    probe_grad = jnp.stack([lax.optimization_barrier(jnp.sum(o_re * g_re + o_im * g_im, 0)), lax.optimization_barrier(jnp.sum(o_re * g_im - o_im * g_re, 0))], 1)
    illumination = lax.optimization_barrier(jnp.sum(windows[:, 0] ** 2 + windows[:, 1] ** 2, 0))
    return (win_grad, probe_grad, illumination, loss_part)

def reference(object_field, probe, amplitude, offsets):
    column, rowwise = dft_tables(PATCH)
    extended = jnp.concatenate([object_field, jnp.zeros((2, TILE, OWIDTH), jnp.float32)], 1)
    block_offsets = offsets.reshape(N_ROW, POS_DEV, 2)
    block_amps = amplitude.reshape(N_ROW, POS_DEV, PATCH, PATCH)

    def cut(row_start, col_start):
        return lax.dynamic_slice(extended, (jnp.int32(0), row_start.astype(jnp.int32), col_start.astype(jnp.int32)), (2, PATCH, PATCH))

    def visit(carry, block):
        grad_ext, probe_sum, illum_sum, loss_sum = carry
        block_off, block_amp = block
        windows = jax.vmap(cut)(block_off[:, 0], block_off[:, 1])
        win_grad, probe_grad, illumination, loss_part = window_terms(windows, probe, block_amp, column, rowwise)

        def add_one(k, grads):
            start = (jnp.int32(0), block_off[k, 0].astype(jnp.int32), block_off[k, 1].astype(jnp.int32))
            current = lax.dynamic_slice(grads, start, (2, PATCH, PATCH))
            return lax.dynamic_update_slice(grads, current + win_grad[k], start)
        grad_ext = lax.fori_loop(0, POS_DEV, add_one, grad_ext)
        return ((grad_ext, probe_sum + probe_grad, illum_sum + illumination, loss_sum + loss_part), None)
    init = (jnp.zeros((2, NROWS + TILE, OWIDTH), jnp.float32), jnp.zeros((MODES, 2, PATCH, PATCH), jnp.float32), jnp.zeros((PATCH, PATCH), jnp.float32), jnp.zeros((), jnp.float32))
    final, unused = lax.scan(visit, init, (block_offsets, block_amps))
    grad_ext, probe_sum, illum_sum, loss_sum = final
    object_grad = grad_ext[:, :NROWS]
    probe_dir = probe_sum / jnp.sqrt(illum_sum + 1.0)[None, None]
    loss = (loss_sum / (POSITIONS * PATCH * PATCH)).reshape(1)
    return (object_grad, probe_dir, loss)
```

```python
import functools
import math

import jax
import jax.numpy as jnp
import ml_dtypes
import numpy as np
from jax import lax
from jax.experimental import pallas as pl
from jax.experimental.pallas import tpu as pltpu
from jax.sharding import PartitionSpec as P

MESH = pl.DeviceIdType.MESH
F32 = jnp.float32
BF16 = jnp.bfloat16


def dft_tables(size):
    idx = np.arange(size)
    angle = (idx[:, None] * idx[None, :] % size) * (2.0 * math.pi / size)
    scale = 1.0 / math.sqrt(size)
    cosine = np.cos(angle) * scale
    sine = np.sin(angle) * scale
    fwd = np.block([[cosine, -sine], [sine, cosine]])
    inv = np.block([[cosine, sine], [-sine, cosine]])
    return fwd.astype(ml_dtypes.bfloat16), inv.astype(ml_dtypes.bfloat16)


def scan_kernel(
    first, offs, lo, hi, probe, amp, fwd, inv, pay_in, loss_in,
    pay, loss, grad, strip, gstrip, window, wave, half, gfar, ghalf,
):
    patch = probe.shape[2]
    modes = probe.shape[0]
    g = pl.program_id(0)

    @pl.when(g == 0)
    def _():
        for comp in range(2):
            for t in range(3):
                strip[comp, t, 0:patch, :] = lo[comp, :, t * 128:(t + 1) * 128]
                strip[comp, t, patch:2 * patch, :] = hi[comp, :, t * 128:(t + 1) * 128]
        gstrip[...] = jnp.zeros_like(gstrip)
        if first:
            pay[...] = jnp.zeros_like(pay)
            loss[...] = jnp.zeros_like(loss)
        else:
            pay[...] = pay_in[...]
            loss[...] = loss_in[...]

    row = offs[g, 0]
    col = offs[g, 1]
    lane = lax.broadcasted_iota(jnp.int32, (patch, 128), 1)
    back = jnp.where(col == 0, 0, 128 - col)
    keep = lane < 128 - col
    groups = patch // 8
    for comp in range(2):
        rolled = [
            pltpu.roll(strip[comp, t, pl.ds(row, patch), :], back, 1) for t in range(3)
        ]
        for h in range(2):
            window[comp, :, h * 128:(h + 1) * 128] = jnp.where(keep, rolled[h], rolled[h + 1])
    for h in range(2):
        cs = slice(h * 128, (h + 1) * 128)
        o_re, o_im = window[0, :, cs], window[1, :, cs]
        pay[h * groups:(h + 1) * groups, 2 * modes] += (o_re * o_re + o_im * o_im).reshape(
            groups, 8, 128
        )
    for m in range(modes):
        rs = slice(m * patch, (m + 1) * patch)
        o_re, o_im = window[0], window[1]
        p_re, p_im = probe[m, 0], probe[m, 1]
        wave[rs, 0:patch] = (p_re * o_re - p_im * o_im).astype(BF16)
        wave[rs, patch:2 * patch] = (p_re * o_im + p_im * o_re).astype(BF16)
    for m in range(modes):
        rs = slice(m * patch, (m + 1) * patch)
        out = jnp.dot(wave[rs, :], fwd[...], preferred_element_type=F32).astype(BF16)
        for comp in range(2):
            for q in range(2):
                half[q, comp * patch:(comp + 1) * patch, m * 128:(m + 1) * 128] = out[
                    :, comp * patch + q * 128:comp * patch + (q + 1) * 128
                ]
    for q in range(2):
        far = jnp.dot(inv[...], half[q], preferred_element_type=F32)
        square = far * far
        power = square[:patch] + square[patch:]
        power = power[:, :128] + power[:, 128:]
        root = lax.rsqrt(power)
        magnitude = jnp.where(power > 0.0, power * root, 0.0)
        a = amp[0, :, q * 128:(q + 1) * 128]
        diff = magnitude - a
        loss[...] += jnp.sum((diff * diff).reshape(groups, 8, 128), 0)
        weight = 0.25 - 0.25 * (a * jnp.minimum(root, 2.0))
        weight = jnp.concatenate([weight, weight], 1)
        weight = jnp.concatenate([weight, weight], 0)
        gfar[q] = (weight * far).astype(BF16)
    for q in range(2):
        out = jnp.dot(fwd[...], gfar[q], preferred_element_type=F32).astype(BF16)
        for comp in range(2):
            for m in range(modes):
                ghalf[
                    m * patch:(m + 1) * patch, comp * patch + q * 128:comp * patch + (q + 1) * 128
                ] = out[comp * patch:(comp + 1) * patch, m * 128:(m + 1) * 128]
    total = [None, None]
    for m in range(modes):
        rs = slice(m * patch, (m + 1) * patch)
        gw = jnp.dot(ghalf[rs, :], inv[...], preferred_element_type=F32)
        g_re, g_im = gw[:, :patch], gw[:, patch:]
        p_re, p_im = probe[m, 0], probe[m, 1]
        o_re, o_im = window[0], window[1]
        terms = (p_re * g_re + p_im * g_im, p_re * g_im - p_im * g_re)
        total = [t if s is None else s + t for s, t in zip(total, terms)]
        for comp, val in enumerate((o_re * g_re + o_im * g_im, o_re * g_im - o_im * g_re)):
            for h in range(2):
                pay[h * groups:(h + 1) * groups, 2 * m + comp] += val[
                    :, h * 128:(h + 1) * 128
                ].reshape(groups, 8, 128)
    ahead = lane >= col
    for comp in range(2):
        left = pltpu.roll(total[comp][:, :128], col, 1)
        right = pltpu.roll(total[comp][:, 128:], col, 1)
        parts = (
            jnp.where(ahead, left, 0.0),
            jnp.where(ahead, right, left),
            jnp.where(ahead, 0.0, right),
        )
        for t in range(3):
            gstrip[comp, t, pl.ds(row, patch), :] += parts[t]

    @pl.when(g == pl.num_programs(0) - 1)
    def _():
        for comp in range(2):
            for t in range(3):
                grad[comp, :, t * 128:(t + 1) * 128] = gstrip[comp, t]


def scan_part(first, offs, lo, hi, probe, amplitude, tables, pay_in, loss_in):
    (lo, lo_block), (hi, hi_block) = lo, hi
    modes, _, patch, _ = probe.shape
    width = lo.shape[2]
    count = offs.shape[0]
    base = 0 if first else count
    whole = lambda shape: pl.BlockSpec(shape, lambda g: (0,) * len(shape))
    pay_shape = (patch // 4, 2 * modes + 1, 8, 128)
    flops = count * 4 * modes * 2 * patch * (2 * patch) ** 2
    return pl.pallas_call(
        functools.partial(scan_kernel, first),
        grid=(count,),
        in_specs=[
            pl.BlockSpec(memory_space=pltpu.SMEM),
            pl.BlockSpec((2, patch, width), lambda g: (0, lo_block, 0)),
            pl.BlockSpec((2, patch, width), lambda g: (0, hi_block, 0)),
            whole(probe.shape),
            pl.BlockSpec((1, patch, patch), lambda g: (g + base, 0, 0)),
            whole(tables[0].shape),
            whole(tables[1].shape),
            whole(pay_in.shape),
            whole(loss_in.shape),
        ],
        out_specs=[whole(pay_shape), whole((8, 128)), whole((2, 2 * patch, width))],
        out_shape=[
            jax.ShapeDtypeStruct(pay_shape, F32),
            jax.ShapeDtypeStruct((8, 128), F32),
            jax.ShapeDtypeStruct((2, 2 * patch, width), F32),
        ],
        scratch_shapes=[
            pltpu.VMEM((2, 3, 2 * patch, 128), F32),
            pltpu.VMEM((2, 3, 2 * patch, 128), F32),
            pltpu.VMEM((2, patch, patch), F32),
            pltpu.VMEM((modes * patch, 2 * patch), BF16),
            pltpu.VMEM((2, 2 * patch, modes * 128), BF16),
            pltpu.VMEM((2, 2 * patch, modes * 128), BF16),
            pltpu.VMEM((modes * patch, 2 * patch), BF16),
        ],
        compiler_params=pltpu.CompilerParams(vmem_limit_bytes=48 << 20),
        cost_estimate=pl.CostEstimate(
            flops=flops, bytes_accessed=6 << 20, transcendentals=count * patch * patch
        ),
        name="scan_first" if first else "scan_second",
    )(offs, lo, hi, probe, amplitude, tables[0], tables[1], pay_in, loss_in)


def sum_kernel(
    n, orders, pay, loss, lower, probe_out, loss_out, carried,
    acc, landed, full, loss_buf, loss_land, halo,
    rs_send, rs_recv, ag_send, ag_recv, loss_send, loss_recv, halo_send, halo_recv,
):
    me = lax.axis_index("row")
    bits = orders[0]
    steps = len(bits)
    planes = pay.shape[1]
    size = pay.shape[0] // len(orders)
    partner = {b: me + b * (1 - 2 * ((me // b) % 2)) for b in bits}

    barrier = pltpu.get_barrier_semaphore()
    for b in bits:
        pl.semaphore_signal(barrier, inc=1, device_id={"row": partner[b]}, device_id_type=MESH)

    @pl.when(me > 0)
    def _():
        pl.semaphore_signal(barrier, inc=1, device_id={"row": me - 1}, device_id_type=MESH)

    @pl.when(me < n - 1)
    def _():
        pl.semaphore_signal(barrier, inc=1, device_id={"row": me + 1}, device_id_type=MESH)

    pl.semaphore_wait(barrier, steps + jnp.minimum(me, 1) + jnp.minimum(n - 1 - me, 1))

    def halo_copy():
        return pltpu.make_async_remote_copy(
            src_ref=lower, dst_ref=halo, send_sem=halo_send, recv_sem=halo_recv,
            device_id={"row": me + 1}, device_id_type=MESH,
        )

    base = [h * size for h in range(len(orders))]
    length = size
    spot = 0
    loss_buf[0] = loss[...]
    for s in range(steps):
        length //= 2
        copies = []
        for h, order in enumerate(orders):
            b = order[s]
            bit = (me // b) % 2
            source = pay if s == 0 else acc
            send_at = base[h] + (1 - bit) * length
            base[h] = base[h] + bit * length
            copy = pltpu.make_async_remote_copy(
                src_ref=source.at[pl.ds(send_at, length)],
                dst_ref=landed.at[h, pl.ds(spot, length)],
                send_sem=rs_send.at[h, s], recv_sem=rs_recv.at[h, s],
                device_id={"row": partner[b]}, device_id_type=MESH,
            )
            copy.start()
            copies.append(copy)
        small = pltpu.make_async_remote_copy(
            src_ref=loss_buf.at[s], dst_ref=loss_land.at[s],
            send_sem=loss_send.at[s], recv_sem=loss_recv.at[s],
            device_id={"row": partner[bits[s]]}, device_id_type=MESH,
        )
        small.start()
        if s == 0:
            @pl.when(me < n - 1)
            def _():
                halo_copy().start()
        for h, copy in enumerate(copies):
            copy.wait()
            source = pay if s == 0 else acc
            acc[pl.ds(base[h], length)] = (
                source[pl.ds(base[h], length)] + landed[h, pl.ds(spot, length)]
            )
        small.wait()
        loss_buf[s + 1] = loss_buf[s] + loss_land[s]
        spot += length
    for h in range(len(orders)):
        own = acc[pl.ds(base[h], length)]
        full[pl.ds(base[h], length)] = own[:, :planes - 1] * lax.rsqrt(own[:, planes - 1:] + 1.0)
    for s in reversed(range(steps)):
        copies = []
        for h, order in enumerate(orders):
            b = order[s]
            bit = (me // b) % 2
            at = pl.ds(base[h], length)
            copy = pltpu.make_async_remote_copy(
                src_ref=full.at[at], dst_ref=full.at[at],
                send_sem=ag_send.at[h, s], recv_sem=ag_recv.at[h, s],
                device_id={"row": partner[b]}, device_id_type=MESH,
            )
            copy.start()
            copies.append(copy)
            base[h] = base[h] - bit * length
        for copy in copies:
            copy.wait()
        length *= 2
    groups = pay.shape[0] // 2
    patch = groups * 8
    for h in range(2):
        for plane in range(planes - 1):
            probe_out[plane // 2, plane % 2, :, h * 128:(h + 1) * 128] = full[
                h * groups:(h + 1) * groups, plane
            ].reshape(patch, 128)
    loss_out[...] = loss_buf[steps]

    @pl.when(me < n - 1)
    def _():
        halo_copy().wait_send()

    @pl.when(me > 0)
    def _():
        halo_copy().wait_recv()
        carried[...] = halo[...]

    @pl.when(me == 0)
    def _():
        carried[...] = jnp.zeros_like(carried)


def sum_parts(pay, loss, strip_grad, probe_shape):
    n = lax.axis_size("row")
    modes, _, patch, _ = probe_shape
    chunks, planes = pay.shape[:2]
    width = strip_grad.shape[2]
    steps = n.bit_length() - 1
    bits = [1 << s for s in range(steps)]
    orders = [bits]
    if chunks >= 2 * n:
        orders = [bits, bits[:1] + bits[2:] + bits[1:2]]
    parts = len(orders)
    vmem = pl.BlockSpec(memory_space=pltpu.VMEM)
    return pl.pallas_call(
        functools.partial(sum_kernel, n, orders),
        grid=(1,),
        in_specs=[vmem, vmem, pl.BlockSpec((2, patch, width), lambda g: (0, 1, 0))],
        out_specs=[vmem, vmem, vmem],
        out_shape=[
            jax.ShapeDtypeStruct(probe_shape, F32),
            jax.ShapeDtypeStruct((8, 128), F32),
            jax.ShapeDtypeStruct((2, patch, width), F32),
        ],
        scratch_shapes=[
            pltpu.VMEM(pay.shape, F32),
            pltpu.VMEM((parts, chunks // parts, planes, 8, 128), F32),
            pltpu.VMEM((chunks, planes - 1, 8, 128), F32),
            pltpu.VMEM((steps + 1, 8, 128), F32),
            pltpu.VMEM((steps, 8, 128), F32),
            pltpu.VMEM((2, patch, width), F32),
            pltpu.SemaphoreType.DMA((parts, steps)),
            pltpu.SemaphoreType.DMA((parts, steps)),
            pltpu.SemaphoreType.DMA((parts, steps)),
            pltpu.SemaphoreType.DMA((parts, steps)),
            pltpu.SemaphoreType.DMA((steps,)),
            pltpu.SemaphoreType.DMA((steps,)),
            pltpu.SemaphoreType.DMA,
            pltpu.SemaphoreType.DMA,
        ],
        compiler_params=pltpu.CompilerParams(
            collective_id=0, has_side_effects=True, vmem_limit_bytes=48 << 20
        ),
        name="sum_parts",
    )(pay, loss, strip_grad)


def per_device(object_field, probe, amplitude, offsets):
    tile = object_field.shape[1]
    modes, _, patch, _ = probe.shape
    count = offsets.shape[0]
    size = lax.axis_size("row")
    tables = tuple(jnp.asarray(t) for t in dft_tables(patch))
    below = lax.ppermute(object_field[:, :patch], "row", [(i + 1, i) for i in range(size - 1)])
    top = lax.axis_index("row") * tile
    near = count // 2
    shift = jnp.array([0] * near + [patch] * (count - near), jnp.int32)
    offs = jnp.stack([offsets[:, 0] - top - shift, offsets[:, 1]], 1)
    none = jnp.zeros((8, 128), F32)
    pay, loss, upper = scan_part(
        True, offs[:near], (object_field, 0), (object_field, 1), probe, amplitude, tables,
        none, none,
    )
    pay, loss, lower = scan_part(
        False, offs[near:], (object_field, 1), (below, 0), probe, amplitude, tables, pay, loss
    )
    probe_dir, loss, carried = sum_parts(pay, loss, lower, probe.shape)
    object_grad = upper + jnp.concatenate([carried, lower[:, :patch]], 1)
    total_pixels = count * size * patch * patch
    return (object_grad, probe_dir, (jnp.sum(loss) / total_pixels).reshape(1))


def solution(mesh):
    placed = (
        P(None, ("groups", "row"), None),
        P(),
        P(("groups", "row"), None, None),
        P(("groups", "row"), None),
    )
    return jax.shard_map(
        per_device,
        mesh=mesh,
        in_specs=placed,
        out_specs=(P(None, ("groups", "row"), None), P("groups", None, None, None), P("groups")),
        check_vma=False,
    )
```

```python
import functools
import math

import jax
import jax.numpy as jnp
import ml_dtypes
import numpy as np
from jax import lax
from jax.experimental import pallas as pl
from jax.experimental.pallas import tpu as pltpu
from jax.sharding import PartitionSpec as P

MESH = pl.DeviceIdType.MESH
F32 = jnp.float32
BF16 = jnp.bfloat16


def dft_tables(size):
    idx = np.arange(size)
    angle = (idx[:, None] * idx[None, :] % size) * (2.0 * math.pi / size)
    scale = 1.0 / math.sqrt(size)
    cosine = np.cos(angle) * scale
    sine = np.sin(angle) * scale
    fwd = np.block([[cosine, -sine], [sine, cosine]])
    inv = np.block([[cosine, sine], [-sine, cosine]])
    return fwd.astype(ml_dtypes.bfloat16), inv.astype(ml_dtypes.bfloat16)


def scan_kernel(
    first, fresh, offs, lo, hi, probe, amp, fwd, inv, pay_in, loss_in, glo_in, ghi_in,
    pay, loss, grad_lo, grad_hi, strip, gstrip, window, wave, half, gfar, ghalf,
):
    patch = probe.shape[2]
    modes = probe.shape[0]
    g = pl.program_id(0)

    @pl.when(g == 0)
    def _():
        for comp in range(2):
            for t in range(3):
                strip[comp, t, 0:patch, :] = lo[comp, :, t * 128:(t + 1) * 128]
                strip[comp, t, patch:2 * patch, :] = hi[comp, :, t * 128:(t + 1) * 128]
                if not fresh:
                    gstrip[comp, t, 0:patch, :] = glo_in[comp, :, t * 128:(t + 1) * 128]
                    gstrip[comp, t, patch:2 * patch, :] = ghi_in[comp, :, t * 128:(t + 1) * 128]
        if fresh:
            gstrip[...] = jnp.zeros_like(gstrip)
        if first:
            pay[...] = jnp.zeros_like(pay)
            loss[...] = jnp.zeros_like(loss)
        else:
            pay[...] = pay_in[...]
            loss[...] = loss_in[...]

    row = offs[g, 0]
    col = offs[g, 1]
    lane = lax.broadcasted_iota(jnp.int32, (patch, 128), 1)
    back = jnp.where(col == 0, 0, 128 - col)
    keep = lane < 128 - col
    groups = patch // 8
    for comp in range(2):
        rolled = [
            pltpu.roll(strip[comp, t, pl.ds(row, patch), :], back, 1) for t in range(3)
        ]
        for h in range(2):
            window[comp, :, h * 128:(h + 1) * 128] = jnp.where(keep, rolled[h], rolled[h + 1])
    for h in range(2):
        cs = slice(h * 128, (h + 1) * 128)
        o_re, o_im = window[0, :, cs], window[1, :, cs]
        pay[h * groups:(h + 1) * groups, 2 * modes] += (o_re * o_re + o_im * o_im).reshape(
            groups, 8, 128
        )
    for m in range(modes):
        rs = slice(m * patch, (m + 1) * patch)
        o_re, o_im = window[0], window[1]
        p_re, p_im = probe[m, 0], probe[m, 1]
        wave[rs, 0:patch] = (p_re * o_re - p_im * o_im).astype(BF16)
        wave[rs, patch:2 * patch] = (p_re * o_im + p_im * o_re).astype(BF16)
    for m in range(modes):
        rs = slice(m * patch, (m + 1) * patch)
        out = jnp.dot(wave[rs, :], fwd[...], preferred_element_type=F32).astype(BF16)
        for comp in range(2):
            for q in range(2):
                half[q, comp * patch:(comp + 1) * patch, m * 128:(m + 1) * 128] = out[
                    :, comp * patch + q * 128:comp * patch + (q + 1) * 128
                ]
    for q in range(2):
        far = jnp.dot(inv[...], half[q], preferred_element_type=F32)
        square = far * far
        power = square[:patch] + square[patch:]
        power = power[:, :128] + power[:, 128:]
        root = lax.rsqrt(power)
        magnitude = jnp.where(power > 0.0, power * root, 0.0)
        a = amp[0, :, q * 128:(q + 1) * 128]
        diff = magnitude - a
        loss[...] += jnp.sum((diff * diff).reshape(groups, 8, 128), 0)
        weight = 0.25 - 0.25 * (a * jnp.minimum(root, 2.0))
        weight = jnp.concatenate([weight, weight], 1)
        weight = jnp.concatenate([weight, weight], 0)
        gfar[q] = (weight * far).astype(BF16)
    for q in range(2):
        out = jnp.dot(fwd[...], gfar[q], preferred_element_type=F32).astype(BF16)
        for comp in range(2):
            for m in range(modes):
                ghalf[
                    m * patch:(m + 1) * patch, comp * patch + q * 128:comp * patch + (q + 1) * 128
                ] = out[comp * patch:(comp + 1) * patch, m * 128:(m + 1) * 128]
    total = [None, None]
    for m in range(modes):
        rs = slice(m * patch, (m + 1) * patch)
        gw = jnp.dot(ghalf[rs, :], inv[...], preferred_element_type=F32)
        g_re, g_im = gw[:, :patch], gw[:, patch:]
        p_re, p_im = probe[m, 0], probe[m, 1]
        o_re, o_im = window[0], window[1]
        terms = (p_re * g_re + p_im * g_im, p_re * g_im - p_im * g_re)
        total = [t if s is None else s + t for s, t in zip(total, terms)]
        for comp, val in enumerate((o_re * g_re + o_im * g_im, o_re * g_im - o_im * g_re)):
            for h in range(2):
                pay[h * groups:(h + 1) * groups, 2 * m + comp] += val[
                    :, h * 128:(h + 1) * 128
                ].reshape(groups, 8, 128)
    ahead = lane >= col
    for comp in range(2):
        left = pltpu.roll(total[comp][:, :128], col, 1)
        right = pltpu.roll(total[comp][:, 128:], col, 1)
        parts = (
            jnp.where(ahead, left, 0.0),
            jnp.where(ahead, right, left),
            jnp.where(ahead, 0.0, right),
        )
        for t in range(3):
            gstrip[comp, t, pl.ds(row, patch), :] += parts[t]

    @pl.when(g == pl.num_programs(0) - 1)
    def _():
        for comp in range(2):
            for t in range(3):
                grad_lo[comp, :, t * 128:(t + 1) * 128] = gstrip[comp, t, 0:patch, :]
                grad_hi[comp, :, t * 128:(t + 1) * 128] = gstrip[comp, t, patch:2 * patch, :]


def scan_part(name, base, offs, lo, hi, probe, amplitude, tables, pay_in, loss_in, glo_in, ghi_in):
    (lo, lo_block), (hi, hi_block) = lo, hi
    modes, _, patch, _ = probe.shape
    width = lo.shape[2]
    count = offs.shape[0]
    first = pay_in.ndim == 2
    fresh = glo_in.ndim == 2
    whole = lambda shape: pl.BlockSpec(shape, lambda g: (0,) * len(shape))
    pay_shape = (patch // 4, 2 * modes + 1, 8, 128)
    flops = count * 4 * modes * 2 * patch * (2 * patch) ** 2
    return pl.pallas_call(
        functools.partial(scan_kernel, first, fresh),
        grid=(count,),
        in_specs=[
            pl.BlockSpec(memory_space=pltpu.SMEM),
            pl.BlockSpec((2, patch, width), lambda g: (0, lo_block, 0)),
            pl.BlockSpec((2, patch, width), lambda g: (0, hi_block, 0)),
            whole(probe.shape),
            pl.BlockSpec((1, patch, patch), lambda g: (g + base, 0, 0)),
            whole(tables[0].shape),
            whole(tables[1].shape),
            whole(pay_in.shape),
            whole(loss_in.shape),
            whole(glo_in.shape),
            whole(ghi_in.shape),
        ],
        out_specs=[whole(pay_shape), whole((8, 128))] + [whole((2, patch, width))] * 2,
        out_shape=[
            jax.ShapeDtypeStruct(pay_shape, F32),
            jax.ShapeDtypeStruct((8, 128), F32),
            jax.ShapeDtypeStruct((2, patch, width), F32),
            jax.ShapeDtypeStruct((2, patch, width), F32),
        ],
        scratch_shapes=[
            pltpu.VMEM((2, 3, 2 * patch, 128), F32),
            pltpu.VMEM((2, 3, 2 * patch, 128), F32),
            pltpu.VMEM((2, patch, patch), F32),
            pltpu.VMEM((modes * patch, 2 * patch), BF16),
            pltpu.VMEM((2, 2 * patch, modes * 128), BF16),
            pltpu.VMEM((2, 2 * patch, modes * 128), BF16),
            pltpu.VMEM((modes * patch, 2 * patch), BF16),
        ],
        compiler_params=pltpu.CompilerParams(vmem_limit_bytes=60 << 20),
        cost_estimate=pl.CostEstimate(
            flops=flops, bytes_accessed=6 << 20, transcendentals=count * patch * patch
        ),
        name=name,
    )(offs, lo, hi, probe, amplitude, tables[0], tables[1], pay_in, loss_in, glo_in, ghi_in)


def sum_kernel(
    n, orders, pay, loss, probe_out, loss_out,
    acc, landed, full, loss_buf, loss_land,
    rs_send, rs_recv, ag_send, ag_recv, loss_send, loss_recv,
):
    me = lax.axis_index("row")
    bits = orders[0]
    steps = len(bits)
    halves = range(len(orders))
    planes = pay.shape[1]
    size = pay.shape[0] // len(orders)
    bit_of = {b: (me // b) % 2 for b in bits}
    partner = {b: me + b * (1 - 2 * bit_of[b]) for b in bits}

    barrier = pltpu.get_barrier_semaphore()
    for b in bits:
        pl.semaphore_signal(barrier, inc=1, device_id={"row": partner[b]}, device_id_type=MESH)
    pl.semaphore_wait(barrier, steps)

    def send(src, dst, send_sem, recv_sem, b):
        copy = pltpu.make_async_remote_copy(
            src_ref=src, dst_ref=dst, send_sem=send_sem, recv_sem=recv_sem,
            device_id={"row": partner[b]}, device_id_type=MESH,
        )
        copy.start()
        return copy

    base = [h * size for h in halves]
    lengths = [size >> s for s in range(steps + 1)]
    spots = [size - lengths[s] for s in range(steps)]

    def scatter(h, s):
        b = orders[h][s]
        length = lengths[s + 1]
        send_at = base[h] + (1 - bit_of[b]) * length
        base[h] = base[h] + bit_of[b] * length
        source = pay if s == 0 else acc
        return send(
            source.at[pl.ds(send_at, length)], landed.at[h, pl.ds(spots[s], length)],
            rs_send.at[h, s], rs_recv.at[h, s], b,
        )

    def gather(h, s):
        b = orders[h][s]
        length = lengths[s + 1]
        at = pl.ds(base[h], length)
        base[h] = base[h] - bit_of[b] * length
        return send(full.at[at], full.at[at], ag_send.at[h, s], ag_recv.at[h, s], b)

    def small(s):
        return send(loss_buf.at[s], loss_land.at[s], loss_send.at[s], loss_recv.at[s], bits[s])

    groups = pay.shape[0] // 2
    flying = [scatter(h, 0) for h in halves]
    loss_buf[0] = loss[...]
    little = small(0)
    for s in range(steps):
        source = pay if s == 0 else acc
        for h in halves:
            flying[h].wait()
            length = lengths[s + 1]
            at = pl.ds(base[h], length)
            total = source[at] + landed[h, pl.ds(spots[s], length)]
            if s < steps - 1:
                acc[at] = total
                flying[h] = scatter(h, s + 1)
            else:
                full[at] = total[:, :planes - 1] * lax.rsqrt(total[:, planes - 1:] + 1.0)
                flying[h] = gather(h, s)
        little.wait()
        loss_buf[s + 1] = loss_buf[s] + loss_land[s]
        if s < steps - 1:
            little = small(s + 1)
    loss_out[...] = loss_buf[steps]
    for s in reversed(range(steps)):
        for h in halves:
            flying[h].wait()
            if s > 0:
                flying[h] = gather(h, s - 1)
    patch = groups * 8
    for h in range(2):
        for plane in range(planes - 1):
            probe_out[plane // 2, plane % 2, :, h * 128:(h + 1) * 128] = full[
                h * groups:(h + 1) * groups, plane
            ].reshape(patch, 128)


def sum_parts(pay, loss, probe_shape):
    n = lax.axis_size("row")
    chunks, planes = pay.shape[:2]
    steps = n.bit_length() - 1
    bits = [1 << s for s in range(steps)]
    orders = [bits]
    if chunks >= 2 * n:
        orders = [bits, bits[:1] + bits[2:3] + bits[1:2] + bits[3:]]
    parts = len(orders)
    vmem = pl.BlockSpec(memory_space=pltpu.VMEM)
    return pl.pallas_call(
        functools.partial(sum_kernel, n, orders),
        in_specs=[vmem, vmem],
        out_specs=[vmem, vmem],
        out_shape=[
            jax.ShapeDtypeStruct(probe_shape, F32),
            jax.ShapeDtypeStruct((8, 128), F32),
        ],
        scratch_shapes=[
            pltpu.VMEM(pay.shape, F32),
            pltpu.VMEM((parts, chunks // parts, planes, 8, 128), F32),
            pltpu.VMEM((chunks, planes - 1, 8, 128), F32),
            pltpu.VMEM((steps + 1, 8, 128), F32),
            pltpu.VMEM((steps, 8, 128), F32),
            pltpu.SemaphoreType.DMA((parts, steps)),
            pltpu.SemaphoreType.DMA((parts, steps)),
            pltpu.SemaphoreType.DMA((parts, steps)),
            pltpu.SemaphoreType.DMA((parts, steps)),
            pltpu.SemaphoreType.DMA((steps,)),
            pltpu.SemaphoreType.DMA((steps,)),
        ],
        compiler_params=pltpu.CompilerParams(
            collective_id=0, has_side_effects=True, vmem_limit_bytes=48 << 20
        ),
        name="sum_parts",
    )(pay, loss)


def per_device(object_field, probe, amplitude, offsets):
    tile = object_field.shape[1]
    modes, _, patch, _ = probe.shape
    count = offsets.shape[0]
    size = lax.axis_size("row")
    tables = tuple(jnp.asarray(t) for t in dft_tables(patch))
    below = lax.ppermute(object_field[:, :patch], "row", [(i + 1, i) for i in range(size - 1)])
    top = lax.axis_index("row") * tile
    near = count // 2
    shift = jnp.array([0] * near + [patch] * (count - near), jnp.int32)
    offs = jnp.stack([offsets[:, 0] - top - shift, offsets[:, 1]], 1)
    none = jnp.zeros((8, 128), F32)
    early = near // 2
    near_field = ((object_field, 0), (object_field, 1), probe, amplitude, tables)
    far_field = ((object_field, 1), (below, 0), probe, amplitude, tables)
    pay, loss, near_lo, near_hi = scan_part(
        "scan_early", 0, offs[:early], *near_field, none, none, none, none
    )
    pay, loss, far_lo, far_hi = scan_part(
        "scan_far", near, offs[near:], *far_field, pay, loss, none, none
    )
    carried = lax.ppermute(far_hi, "row", [(i, i + 1) for i in range(size - 1)])
    pay, loss, near_lo, near_hi = scan_part(
        "scan_late", early, offs[early:near], *near_field, pay, loss, near_lo, near_hi
    )
    probe_dir, loss = sum_parts(pay, loss, probe.shape)
    object_grad = jnp.concatenate([near_lo + carried, near_hi + far_lo], 1)
    total_pixels = count * size * patch * patch
    return (object_grad, probe_dir, (jnp.sum(loss) / total_pixels).reshape(1))


def solution(mesh):
    placed = (
        P(None, ("groups", "row"), None),
        P(),
        P(("groups", "row"), None, None),
        P(("groups", "row"), None),
    )
    return jax.shard_map(
        per_device,
        mesh=mesh,
        in_specs=placed,
        out_specs=(P(None, ("groups", "row"), None), P("groups", None, None, None), P("groups")),
        check_vma=False,
    )
```

```python
import functools
import math

import jax
import jax.numpy as jnp
import ml_dtypes
import numpy as np
from jax import lax
from jax.experimental import pallas as pl
from jax.experimental.pallas import tpu as pltpu
from jax.sharding import PartitionSpec as P

MESH = pl.DeviceIdType.MESH
F32 = jnp.float32
BF16 = jnp.bfloat16


def dft_tables(size):
    idx = np.arange(size)
    angle = (idx[:, None] * idx[None, :] % size) * (2.0 * math.pi / size)
    scale = 1.0 / math.sqrt(size)
    cosine = np.cos(angle) * scale
    sine = np.sin(angle) * scale
    fwd = np.block([[cosine, -sine], [sine, cosine]])
    inv = np.block([[cosine, sine], [-sine, cosine]])
    return fwd.astype(ml_dtypes.bfloat16), inv.astype(ml_dtypes.bfloat16)


def scan_kernel(
    first, offs, lo, hi, probe, amp, fwd, inv, pay_in, loss_in, pay, loss, *rest
):
    grads, (strip, gstrip, window, wave, half, gfar, ghalf) = rest[:-7], rest[-7:]
    patch = probe.shape[2]
    modes = probe.shape[0]
    g = pl.program_id(0)

    @pl.when(g == 0)
    def _():
        for comp in range(2):
            for t in range(3):
                strip[comp, t, 0:patch, :] = lo[comp, :, t * 128:(t + 1) * 128]
                strip[comp, t, patch:2 * patch, :] = hi[comp, :, t * 128:(t + 1) * 128]
        gstrip[...] = jnp.zeros_like(gstrip)
        if first:
            pay[...] = jnp.zeros_like(pay)
            loss[...] = jnp.zeros_like(loss)
        else:
            pay[...] = pay_in[...]
            loss[...] = loss_in[...]

    row = offs[g, 0]
    col = offs[g, 1]
    lane = lax.broadcasted_iota(jnp.int32, (patch, 128), 1)
    back = jnp.where(col == 0, 0, 128 - col)
    keep = lane < 128 - col
    groups = patch // 8
    for comp in range(2):
        rolled = [
            pltpu.roll(strip[comp, t, pl.ds(row, patch), :], back, 1) for t in range(3)
        ]
        for h in range(2):
            window[comp, :, h * 128:(h + 1) * 128] = jnp.where(keep, rolled[h], rolled[h + 1])
    for h in range(2):
        cs = slice(h * 128, (h + 1) * 128)
        o_re, o_im = window[0, :, cs], window[1, :, cs]
        pay[h * groups:(h + 1) * groups, 2 * modes] += (o_re * o_re + o_im * o_im).reshape(
            groups, 8, 128
        )
    for m in range(modes):
        rs = slice(m * patch, (m + 1) * patch)
        o_re, o_im = window[0], window[1]
        p_re, p_im = probe[m, 0], probe[m, 1]
        wave[rs, 0:patch] = (p_re * o_re - p_im * o_im).astype(BF16)
        wave[rs, patch:2 * patch] = (p_re * o_im + p_im * o_re).astype(BF16)
    for m in range(modes):
        rs = slice(m * patch, (m + 1) * patch)
        out = jnp.dot(wave[rs, :], fwd[...], preferred_element_type=F32).astype(BF16)
        for comp in range(2):
            for q in range(2):
                half[q, comp * patch:(comp + 1) * patch, m * 128:(m + 1) * 128] = out[
                    :, comp * patch + q * 128:comp * patch + (q + 1) * 128
                ]
    for q in range(2):
        far = jnp.dot(inv[...], half[q], preferred_element_type=F32)
        square = far * far
        power = square[:patch] + square[patch:]
        power = power[:, :128] + power[:, 128:]
        root = lax.rsqrt(power)
        magnitude = jnp.where(power > 0.0, power * root, 0.0)
        a = amp[0, :, q * 128:(q + 1) * 128]
        diff = magnitude - a
        loss[...] += jnp.sum((diff * diff).reshape(groups, 8, 128), 0)
        weight = 0.25 - 0.25 * (a * jnp.minimum(root, 2.0))
        weight = jnp.concatenate([weight, weight], 1)
        weight = jnp.concatenate([weight, weight], 0)
        gfar[q] = (weight * far).astype(BF16)
    for q in range(2):
        out = jnp.dot(fwd[...], gfar[q], preferred_element_type=F32).astype(BF16)
        for comp in range(2):
            for m in range(modes):
                ghalf[
                    m * patch:(m + 1) * patch, comp * patch + q * 128:comp * patch + (q + 1) * 128
                ] = out[comp * patch:(comp + 1) * patch, m * 128:(m + 1) * 128]
    total = [None, None]
    for m in range(modes):
        rs = slice(m * patch, (m + 1) * patch)
        gw = jnp.dot(ghalf[rs, :], inv[...], preferred_element_type=F32)
        g_re, g_im = gw[:, :patch], gw[:, patch:]
        p_re, p_im = probe[m, 0], probe[m, 1]
        o_re, o_im = window[0], window[1]
        terms = (p_re * g_re + p_im * g_im, p_re * g_im - p_im * g_re)
        total = [t if s is None else s + t for s, t in zip(total, terms)]
        for comp, val in enumerate((o_re * g_re + o_im * g_im, o_re * g_im - o_im * g_re)):
            for h in range(2):
                pay[h * groups:(h + 1) * groups, 2 * m + comp] += val[
                    :, h * 128:(h + 1) * 128
                ].reshape(groups, 8, 128)
    ahead = lane >= col
    for comp in range(2):
        left = pltpu.roll(total[comp][:, :128], col, 1)
        right = pltpu.roll(total[comp][:, 128:], col, 1)
        parts = (
            jnp.where(ahead, left, 0.0),
            jnp.where(ahead, right, left),
            jnp.where(ahead, 0.0, right),
        )
        for t in range(3):
            gstrip[comp, t, pl.ds(row, patch), :] += parts[t]

    @pl.when(g == pl.num_programs(0) - 1)
    def _():
        for comp in range(2):
            for t in range(3):
                for i, grad in enumerate(grads):
                    rows = grad.shape[1]
                    grad[comp, :, t * 128:(t + 1) * 128] = gstrip[
                        comp, t, i * rows:(i + 1) * rows, :
                    ]


def scan_part(name, base, offs, lo, hi, probe, amplitude, tables, pay_in, loss_in):
    (lo, lo_block), (hi, hi_block) = lo, hi
    modes, _, patch, _ = probe.shape
    width = lo.shape[2]
    count = offs.shape[0]
    first = pay_in.ndim == 2
    grad_shapes = [(2, 2 * patch, width)] if first else [(2, patch, width)] * 2
    whole = lambda shape: pl.BlockSpec(shape, lambda g: (0,) * len(shape))
    pay_shape = (patch // 4, 2 * modes + 1, 8, 128)
    flops = count * 4 * modes * 2 * patch * (2 * patch) ** 2
    return pl.pallas_call(
        functools.partial(scan_kernel, first),
        grid=(count,),
        in_specs=[
            pl.BlockSpec(memory_space=pltpu.SMEM),
            pl.BlockSpec((2, patch, width), lambda g: (0, lo_block, 0)),
            pl.BlockSpec((2, patch, width), lambda g: (0, hi_block, 0)),
            whole(probe.shape),
            pl.BlockSpec((1, patch, patch), lambda g: (g + base, 0, 0)),
            whole(tables[0].shape),
            whole(tables[1].shape),
            whole(pay_in.shape),
            whole(loss_in.shape),
        ],
        out_specs=[whole(pay_shape), whole((8, 128))] + [whole(shape) for shape in grad_shapes],
        out_shape=[
            jax.ShapeDtypeStruct(pay_shape, F32),
            jax.ShapeDtypeStruct((8, 128), F32),
        ]
        + [jax.ShapeDtypeStruct(shape, F32) for shape in grad_shapes],
        scratch_shapes=[
            pltpu.VMEM((2, 3, 2 * patch, 128), F32),
            pltpu.VMEM((2, 3, 2 * patch, 128), F32),
            pltpu.VMEM((2, patch, patch), F32),
            pltpu.VMEM((modes * patch, 2 * patch), BF16),
            pltpu.VMEM((2, 2 * patch, modes * 128), BF16),
            pltpu.VMEM((2, 2 * patch, modes * 128), BF16),
            pltpu.VMEM((modes * patch, 2 * patch), BF16),
        ],
        compiler_params=pltpu.CompilerParams(vmem_limit_bytes=48 << 20),
        cost_estimate=pl.CostEstimate(
            flops=flops, bytes_accessed=6 << 20, transcendentals=count * patch * patch
        ),
        name=name,
    )(offs, lo, hi, probe, amplitude, tables[0], tables[1], pay_in, loss_in)


def sum_kernel(
    n, orders, pay, loss, probe_out, loss_out,
    acc, landed, full, loss_buf, loss_land,
    rs_send, rs_recv, ag_send, ag_recv, loss_send, loss_recv,
):
    me = lax.axis_index("row")
    bits = orders[0]
    steps = len(bits)
    halves = range(len(orders))
    planes = pay.shape[1]
    size = pay.shape[0] // len(orders)
    bit_of = {b: (me // b) % 2 for b in bits}
    partner = {b: me + b * (1 - 2 * bit_of[b]) for b in bits}

    barrier = pltpu.get_barrier_semaphore()
    for b in bits:
        pl.semaphore_signal(barrier, inc=1, device_id={"row": partner[b]}, device_id_type=MESH)
    pl.semaphore_wait(barrier, steps)

    def send(src, dst, send_sem, recv_sem, b):
        copy = pltpu.make_async_remote_copy(
            src_ref=src, dst_ref=dst, send_sem=send_sem, recv_sem=recv_sem,
            device_id={"row": partner[b]}, device_id_type=MESH,
        )
        copy.start()
        return copy

    base = [h * size for h in halves]
    lengths = [size >> s for s in range(steps + 1)]
    spots = [size - lengths[s] for s in range(steps)]

    def scatter(h, s):
        b = orders[h][s]
        length = lengths[s + 1]
        send_at = base[h] + (1 - bit_of[b]) * length
        base[h] = base[h] + bit_of[b] * length
        source = pay if s == 0 else acc
        return send(
            source.at[pl.ds(send_at, length)], landed.at[h, pl.ds(spots[s], length)],
            rs_send.at[h, s], rs_recv.at[h, s], b,
        )

    def gather(h, s):
        b = orders[h][s]
        length = lengths[s + 1]
        at = pl.ds(base[h], length)
        base[h] = base[h] - bit_of[b] * length
        return send(full.at[at], full.at[at], ag_send.at[h, s], ag_recv.at[h, s], b)

    def small(s):
        return send(loss_buf.at[s], loss_land.at[s], loss_send.at[s], loss_recv.at[s], bits[s])

    groups = pay.shape[0] // 2
    flying = [scatter(h, 0) for h in halves]
    loss_buf[0] = loss[...]
    little = small(0)
    for s in range(steps):
        source = pay if s == 0 else acc
        for h in halves:
            flying[h].wait()
            length = lengths[s + 1]
            at = pl.ds(base[h], length)
            total = source[at] + landed[h, pl.ds(spots[s], length)]
            if s < steps - 1:
                acc[at] = total
                flying[h] = scatter(h, s + 1)
            else:
                full[at] = total[:, :planes - 1] * lax.rsqrt(total[:, planes - 1:] + 1.0)
                flying[h] = gather(h, s)
        little.wait()
        loss_buf[s + 1] = loss_buf[s] + loss_land[s]
        if s < steps - 1:
            little = small(s + 1)
    loss_out[...] = loss_buf[steps]
    for s in reversed(range(steps)):
        for h in halves:
            flying[h].wait()
            if s > 0:
                flying[h] = gather(h, s - 1)
    patch = groups * 8
    for h in range(2):
        for plane in range(planes - 1):
            probe_out[plane // 2, plane % 2, :, h * 128:(h + 1) * 128] = full[
                h * groups:(h + 1) * groups, plane
            ].reshape(patch, 128)


def sum_parts(pay, loss, probe_shape):
    n = lax.axis_size("row")
    chunks, planes = pay.shape[:2]
    steps = n.bit_length() - 1
    bits = [1 << s for s in range(steps)]
    orders = [bits]
    if chunks >= 2 * n:
        orders = [bits, bits[:1] + bits[2:3] + bits[1:2] + bits[3:]]
    parts = len(orders)
    vmem = pl.BlockSpec(memory_space=pltpu.VMEM)
    return pl.pallas_call(
        functools.partial(sum_kernel, n, orders),
        in_specs=[vmem, vmem],
        out_specs=[vmem, vmem],
        out_shape=[
            jax.ShapeDtypeStruct(probe_shape, F32),
            jax.ShapeDtypeStruct((8, 128), F32),
        ],
        scratch_shapes=[
            pltpu.VMEM(pay.shape, F32),
            pltpu.VMEM((parts, chunks // parts, planes, 8, 128), F32),
            pltpu.VMEM((chunks, planes - 1, 8, 128), F32),
            pltpu.VMEM((steps + 1, 8, 128), F32),
            pltpu.VMEM((steps, 8, 128), F32),
            pltpu.SemaphoreType.DMA((parts, steps)),
            pltpu.SemaphoreType.DMA((parts, steps)),
            pltpu.SemaphoreType.DMA((parts, steps)),
            pltpu.SemaphoreType.DMA((parts, steps)),
            pltpu.SemaphoreType.DMA((steps,)),
            pltpu.SemaphoreType.DMA((steps,)),
        ],
        compiler_params=pltpu.CompilerParams(
            collective_id=0, has_side_effects=True, vmem_limit_bytes=48 << 20
        ),
        name="sum_parts",
    )(pay, loss)


def per_device(object_field, probe, amplitude, offsets):
    tile = object_field.shape[1]
    modes, _, patch, _ = probe.shape
    count = offsets.shape[0]
    size = lax.axis_size("row")
    tables = tuple(jnp.asarray(t) for t in dft_tables(patch))
    below = lax.ppermute(object_field[:, :patch], "row", [(i + 1, i) for i in range(size - 1)])
    top = lax.axis_index("row") * tile
    near = count // 2
    shift = jnp.array([0] * near + [patch] * (count - near), jnp.int32)
    offs = jnp.stack([offsets[:, 0] - top - shift, offsets[:, 1]], 1)
    none = jnp.zeros((8, 128), F32)
    pay, loss, upper = scan_part(
        "scan_near", 0, offs[:near], (object_field, 0), (object_field, 1), probe, amplitude,
        tables, none, none,
    )
    pay, loss, middle, lower = scan_part(
        "scan_far", near, offs[near:], (object_field, 1), (below, 0), probe, amplitude,
        tables, pay, loss,
    )
    carried = lax.ppermute(lower, "row", [(i, i + 1) for i in range(size - 1)])
    probe_dir, loss = sum_parts(pay, loss, probe.shape)
    object_grad = upper + jnp.concatenate([carried, middle], 1)
    total_pixels = count * size * patch * patch
    return (object_grad, probe_dir, (jnp.sum(loss) / total_pixels).reshape(1))


def solution(mesh):
    placed = (
        P(None, ("groups", "row"), None),
        P(),
        P(("groups", "row"), None, None),
        P(("groups", "row"), None),
    )
    return jax.shard_map(
        per_device,
        mesh=mesh,
        in_specs=placed,
        out_specs=(P(None, ("groups", "row"), None), P("groups", None, None, None), P("groups")),
        check_vma=False,
    )
```
